32 devices in a mesh: row: 8 (over z, y), col: 4 (over x, core).
Axes of the slice: x: 2, y: 2, z: 4, core: 2. Of those that a mesh axis runs over, the one named last changes fastest.
Arguments:
- hidden: bfloat16 [64, 4096], P('row'), may hold values from -6 to 6
- queries: bfloat16 [64, 64, 128], P(('row', 'col')), may hold values from -6 to 6
- keys: bfloat16 [64, 4, 64, 128], P(('row', 'col')), may hold values from -6 to 6
- values: bfloat16 [64, 4, 64, 128], P(('row', 'col')), may hold values from -12 to 12
- out_proj: bfloat16 [8192, 4096], P('col'), may hold values from -0.0625 to 0.0625
- norm_gain: float32 [4096], replicated, may hold values from 0.4 to 1.6
- routes: int32 [64, 8], P('row'), may hold values from 0 to 127, all different within a row; in each aligned block of 8 rows (0 to 7, 8 to 15, ...) at most 8 rows name the same one
- route_probs: float32 [64, 8], P('row'), may hold values from 0.05 to 1
- w_gate: bfloat16 [4096, 131072], P(None, ('row', 'col')), may hold values from -0.09375 to 0.09375
- w_up: bfloat16 [4096, 131072], P(None, ('row', 'col')), may hold values from -0.09375 to 0.09375
- w_down: bfloat16 [131072, 4096], P(('row', 'col')), may hold values from -0.1875 to 0.1875
Outputs:
- updated: bfloat16 [64, 4096], P(('row', 'col'))
The draws below stay inside these ranges and needn't reach their ends.
Inputs may be any that keep to these rules, and one draw needn't show every extreme that they name: `routes`: each row names 8 different experts. In each aligned block of 8 rows (the requests of one index of row) no expert is named by more than 8 rows.
All inputs are finite; a program needn't handle non-finite values.
Results may differ from the reference program's by a relative error of at most 0.017.
Values may be sent and summed in bfloat16 or wider, within the bound.
A program may use at most 256 MiB of HBM per device.

```python
import math
import jax
import jax.numpy as jnp
import numpy as np
from jax import lax

D = 4096
HEADS = 64
KVH = 4
HD = 128
EXPERTS = 128
TOP = 8
FF = 1024
LEN = 64
TOKENS = 64
BLOCK = 8
CAP = 8
N_ROW = 8
DEVICES = 32


def shared_attention(key):
    base = jax.random.fold_in(key, 7)
    query_key, cache_key = jax.random.split(base, 2)
    query_draw = jnp.clip(jax.random.normal(query_key, (TOKENS, HEADS, HD), jnp.float32), -4.0, 4.0)
    cache_draw = jnp.clip(jax.random.normal(cache_key, (TOKENS, KVH, LEN, HD), jnp.float32), -4.0, 4.0)
    return (query_draw, cache_draw)


def draw_queries(key, part):
    return shared_attention(key)[0].astype(jnp.bfloat16)


def draw_keys(key, part):
    return shared_attention(key)[1].astype(jnp.bfloat16)


def level_of(key, dims, cuts, least, largest):
    factor_of = 1.0
    for axis_at, blocks in cuts:
        heights = jax.random.uniform(jax.random.fold_in(jax.random.fold_in(key, 6), axis_at), (blocks,), jnp.float32, least / len(cuts), largest / len(cuts))
        factor_of = factor_of * jnp.repeat(jnp.exp(heights), dims[axis_at] // blocks).reshape((-1,) + (1,) * (len(dims) - 1 - axis_at))
    return factor_of


def assign_block(key, own, number, rows, amount, top, bound, lean):
    sequence = jax.random.permutation(key, amount)
    crowded, common = load_shares(amount, rows * top, bound, lean, True), load_shares(amount, rows * top, bound, lean, False)
    places = jnp.arange(amount)

    def named(lengths, rotation):
        used = int((lengths > 0).sum())
        fixed = max(1, used // 4)
        passed = fixed + (places - fixed + rotation * (used - fixed)) % max(1, amount - fixed)
        return jnp.zeros((amount,), jnp.int32).at[sequence[jnp.where(places < fixed, places, passed)]].set(jnp.asarray(lengths, jnp.int32))

    lengths = jnp.where(number % 4 == 0, named(crowded, number // 4), named(common, number - number // 4 - 1))
    mixed = jax.random.permutation(jax.random.fold_in(own, 3), amount)
    giver, sink = mixed[0:amount // 2 * 2:2], mixed[1:amount // 2 * 2:2]
    room = jnp.minimum(lengths[giver] - 1, bound - lengths[sink]) // 2
    room = jnp.where((giver == sequence[0]) | (sink == sequence[0]) | (lengths[sink] == 0), 0, jnp.maximum(room, 0))
    passed = jax.random.randint(jax.random.fold_in(own, 4), (amount // 2,), 0, 1 << 20) % (room + 1)
    lengths = lengths.at[giver].add(-passed).at[sink].add(passed)
    labels = jnp.searchsorted(jnp.cumsum(lengths), jnp.arange(rows * top), side="right").astype(jnp.int32)
    grid = labels.reshape(top, rows).T
    grid = grid[jax.random.permutation(jax.random.fold_in(own, 1), rows)]
    rotation = jax.random.randint(jax.random.fold_in(own, 2), (rows, 1), 0, top)
    return jnp.take_along_axis(grid, (jnp.arange(top)[None, :] + rotation) % top, axis=1)


def load_shares(number_of, total, bound, lean, full):
    portions = [(1 << 20) // math.isqrt(grade ** lean) + 1 for grade in range(1, number_of + 1)]
    largest = bound if full else min(bound, max(-(-total // number_of), total * portions[0] // sum(portions)))
    least = 1 if total - largest >= number_of - 1 else 0
    counts, spare = [largest] + [least] * (number_of - 1), total - largest - least * (number_of - 1)
    while spare > 0:
        free = [i for i in range(1, number_of) if counts[i] < largest] or [i for i in range(1, number_of) if counts[i] < bound]
        whole, budget = sum([portions[i] for i in free]), spare
        for i in free:
            extra = min(bound - counts[i], max(1, budget * portions[i] // whole), spare)
            counts[i] = counts[i] + extra
            spare = spare - extra
    return np.array(counts)


def noise(own_key, shape, width, limit, shards=(), kind=jnp.bfloat16):
    loudness = level_of(own_key, shape, shards, -0.22, 0.18) if shards else 1.0
    entries = jax.random.normal(own_key, shape, jnp.float32) * width * loudness
    return jnp.minimum(jnp.maximum(entries, -limit), limit).astype(kind)


def setup_inputs(seed: int = 0) -> dict:
    splits = jax.random.split(jax.random.key(seed), 12)
    hidden = noise(splits[0], (TOKENS, D), 1.0, 6.0, ((0, 8),))
    queries = draw_queries(jax.random.fold_in(splits[11], 71), 0)
    keys = draw_keys(jax.random.fold_in(splits[11], 71), 0)
    values = noise(splits[3], (TOKENS, KVH, LEN, HD), 2.0, 12.0, ((0, 32),))
    out_proj = noise(splits[4], (HEADS * HD, D), (HEADS * HD) ** -0.5, 0.0625, ((0, 4),))
    norm_gain = jnp.clip(1.0 + 0.12 * jax.random.normal(splits[5], (D,), jnp.float32), 0.4, 1.6)
    routes_keys = jax.random.split(jax.random.fold_in(splits[6], 1), TOKENS // BLOCK)
    routes_turns = jax.random.permutation(jax.random.fold_in(splits[6], 3), TOKENS // BLOCK)
    routes = jax.vmap(lambda own, number: assign_block(jax.random.fold_in(splits[6], 2), own, number, BLOCK, EXPERTS, TOP, CAP, 2))(routes_keys, routes_turns).reshape((TOKENS, TOP))
    route_probs = jnp.clip(jnp.exp(math.log(1.0) - 2.9957323 * jax.random.uniform(splits[7], (TOKENS, TOP), jnp.float32) ** level_of(splits[7], (TOKENS, TOP), ((0, 8),), -0.2, 0.2)), 0.05, 1.0)
    w_gate = noise(splits[8], (D, EXPERTS * FF), D ** -0.5, 0.09375, ((1, 32),))
    w_up = noise(splits[9], (D, EXPERTS * FF), D ** -0.5, 0.09375, ((1, 32),))
    w_down = noise(splits[10], (EXPERTS * FF, D), FF ** -0.5, 0.1875, ((0, 32),))
    return dict(hidden=hidden, queries=queries, keys=keys, values=values, out_proj=out_proj, norm_gain=norm_gain, routes=routes, route_probs=route_probs, w_gate=w_gate, w_up=w_up, w_down=w_down)


def normalize(resid, norm_gain):
    mean_square = lax.optimization_barrier(jnp.mean(resid * resid, axis=-1, keepdims=True))
    return (resid * lax.rsqrt(mean_square + 1e-06) * norm_gain).astype(jnp.bfloat16)

def reference(hidden, queries, keys, values, out_proj, norm_gain, routes, route_probs, w_gate, w_up, w_down):
    group = HEADS // KVH
    grouped = queries.astype(jnp.float32).reshape(TOKENS, KVH, group, HD)
    scores = jnp.einsum('tgqd,tgpd->tgqp', grouped, keys.astype(jnp.float32)) / math.sqrt(HD)
    attn_weights = jax.nn.softmax(scores, axis=-1).astype(jnp.bfloat16)
    context = jnp.einsum('tgqp,tgpd->tgqd', attn_weights.astype(jnp.float32), values.astype(jnp.float32))
    context = context.astype(jnp.bfloat16).reshape(TOKENS, HEADS * HD)
    attn = jnp.dot(context, out_proj, preferred_element_type=jnp.float32)
    resid = hidden.astype(jnp.float32) + attn
    normed = normalize(resid, norm_gain)
    route_weight = (route_probs / lax.optimization_barrier(jnp.sum(route_probs, axis=-1, keepdims=True))).astype(jnp.bfloat16)
    hid_dev = EXPERTS * FF // DEVICES
    slice_width = min(FF, hid_dev)
    pieces = FF // slice_width
    blocks = normed.reshape(N_ROW, BLOCK, D).astype(jnp.float32)
    slot_ids = jnp.arange(CAP, dtype=jnp.int32)

    def one_expert(total, expert):
        match = routes == expert
        hits = jnp.any(match, axis=-1).astype(jnp.int32).reshape(N_ROW, BLOCK)
        chosen = lax.optimization_barrier(jnp.sum(jnp.where(match, route_weight.astype(jnp.float32), 0.0), axis=-1)).reshape(N_ROW, BLOCK)
        before = jnp.cumsum(hits, axis=1) - hits
        place = ((hits[:, None, :] == 1) & (before[:, None, :] == slot_ids[None, :, None])).astype(jnp.float32)
        arrived = jnp.einsum('rkt,rtd->rkd', place, blocks).astype(jnp.bfloat16).astype(jnp.float32)
        gate_cols = lax.dynamic_slice_in_dim(w_gate, expert * FF, FF, 1).astype(jnp.float32)
        up_cols = lax.dynamic_slice_in_dim(w_up, expert * FF, FF, 1).astype(jnp.float32)
        gate = jnp.einsum('rkd,df->rkf', arrived, gate_cols)
        upward = jnp.einsum('rkd,df->rkf', arrived, up_cols)
        act = (jax.nn.silu(gate) * upward).astype(jnp.bfloat16).astype(jnp.float32)
        act = act.reshape(N_ROW, CAP, pieces, slice_width)
        down_rows = lax.dynamic_slice_in_dim(w_down, expert * FF, FF, 0).astype(jnp.float32)
        down_rows = down_rows.reshape(pieces, slice_width, D)
        piece = jnp.einsum('rkse,sed->rksd', act, down_rows).astype(jnp.bfloat16).astype(jnp.float32)
        scaled = place * chosen[:, None, :]
        added = jnp.einsum('rkt,rksd->rtd', scaled, piece)
        return (total + added, None)
    start = jnp.zeros((N_ROW, BLOCK, D), jnp.float32)
    total, _ = lax.scan(one_expert, start, jnp.arange(EXPERTS, dtype=jnp.int32))
    mixture = total.reshape(TOKENS, D)
    return (resid + mixture).astype(jnp.bfloat16)
```

```python
import math

import jax
import jax.numpy as jnp
from jax import lax
from jax.sharding import PartitionSpec as P

FF = 1024
CAP = 8


def normalize(resid, norm_gain):
    mean_square = jnp.mean(resid * resid, axis=-1, keepdims=True)
    return (resid * lax.rsqrt(mean_square + 1e-06) * norm_gain).astype(jnp.bfloat16)


def gather(block, axis, count):
    copies = jnp.broadcast_to(block[None], (count,) + block.shape)
    return lax.all_to_all(copies, axis, split_axis=0, concat_axis=0, tiled=True)


def shards(
    hidden, queries, keys, values, out_proj, norm_gain, routes, route_probs, w_gate, w_up, w_down
):
    row_count = lax.axis_size("row")
    col_count = lax.axis_size("col")
    col_id = lax.axis_index("col")
    tok_dev = queries.shape[0]
    heads = queries.shape[1]
    head_dim = queries.shape[2]
    kv_heads = keys.shape[1]
    group = heads // kv_heads
    d_model = w_gate.shape[0]
    hid_dev = w_gate.shape[1]
    grouped = queries.reshape(tok_dev, kv_heads, group, head_dim)
    scores = jnp.einsum(
        "tgqd,tgpd->tgqp", grouped, keys, preferred_element_type=jnp.float32
    ) / math.sqrt(head_dim)
    attn_weights = jax.nn.softmax(scores, axis=-1).astype(jnp.bfloat16)
    context = jnp.einsum(
        "tgqp,tgpd->tgqd", attn_weights, values, preferred_element_type=jnp.float32
    )
    context = context.astype(jnp.bfloat16).reshape(tok_dev, heads * head_dim)
    head_rows = lax.all_to_all(context, "col", split_axis=1, concat_axis=0, tiled=True)
    partial_sum = jnp.dot(head_rows, out_proj, preferred_element_type=jnp.float32)
    route_weight = (route_probs / jnp.sum(route_probs, axis=-1, keepdims=True)).astype(jnp.bfloat16)
    exp_local = max(1, hid_dev // FF)
    slice_width = hid_dev // exp_local
    dest_rows = jnp.arange(row_count, dtype=jnp.int32)
    experts_at = (dest_rows[:, None] * col_count + col_id) * hid_dev // FF
    experts_at = experts_at + jnp.arange(exp_local, dtype=jnp.int32)[None, :]
    match = routes[:, :, None, None] == experts_at[None, None, :, :]
    hits = jnp.any(match, axis=1).astype(jnp.int32)
    chosen = jnp.sum(
        jnp.where(match, route_weight[:, :, None, None], jnp.zeros((), jnp.bfloat16)), axis=1
    )
    if routes.shape[0] <= CAP:
        spread = lax.all_to_all(
            jnp.transpose(chosen, (1, 0, 2)).astype(jnp.float32),
            "row", split_axis=0, concat_axis=0, tiled=True,
        )
        spread = spread.reshape(row_count, col_count, tok_dev, exp_local)
        spread = jnp.transpose(spread, (1, 0, 2, 3)).reshape(-1, exp_local)
        parts = partial_sum.astype(jnp.bfloat16).reshape(col_count, tok_dev, d_model)
        parts = lax.all_to_all(parts, "col", split_axis=0, concat_axis=0, tiled=True)
        attn = jnp.sum(parts.astype(jnp.float32), axis=0)
        own = lax.dynamic_slice_in_dim(hidden, col_id * tok_dev, tok_dev, 0)
        resid = own.astype(jnp.float32) + attn
        normed = normalize(resid, norm_gain)
        normed = gather(gather(normed, "row", row_count).reshape(-1, d_model), "col", col_count)
        normed = normed.reshape(-1, d_model)
        gate = jnp.dot(normed, w_gate, preferred_element_type=jnp.float32)
        upward = jnp.dot(normed, w_up, preferred_element_type=jnp.float32)
        widen = jnp.arange(exp_local)[:, None] == jnp.arange(hid_dev)[None, :] // slice_width
        scale = jnp.dot(
            spread.astype(jnp.bfloat16),
            widen.astype(jnp.bfloat16),
            preferred_element_type=jnp.float32,
        )
        act = (jax.nn.silu(gate) * upward * scale).astype(jnp.bfloat16)
        down = jnp.dot(act, w_down, preferred_element_type=jnp.float32).astype(jnp.bfloat16)
        down = down.reshape(col_count, -1, d_model)
        down = lax.all_to_all(down, "col", split_axis=0, concat_axis=0, tiled=True)
        down = jnp.sum(down.astype(jnp.float32), axis=0).astype(jnp.bfloat16)
        down = down.reshape(row_count, tok_dev, d_model)
        down = lax.all_to_all(down, "row", split_axis=0, concat_axis=0, tiled=True)
        mixture = jnp.sum(down.astype(jnp.float32), axis=0)
        return (resid + mixture).astype(jnp.bfloat16)
    attn = lax.psum(partial_sum.astype(jnp.bfloat16), "col").astype(jnp.float32)
    row_resid = hidden.astype(jnp.float32) + attn
    normed = normalize(row_resid, norm_gain)
    resid = lax.dynamic_slice_in_dim(row_resid, col_id * tok_dev, tok_dev, 0)
    before = jnp.cumsum(hits, axis=0) - hits
    hits_t = jnp.transpose(hits, (1, 2, 0))
    before_t = jnp.transpose(before, (1, 2, 0))
    slot_ids = jnp.arange(CAP, dtype=jnp.int32)
    place = (hits_t[:, :, None, :] == 1) & (
        before_t[:, :, None, :] == slot_ids[None, None, :, None]
    )
    place = place.astype(jnp.bfloat16)
    gate_local = w_gate.reshape(d_model, exp_local, slice_width)
    up_local = w_up.reshape(d_model, exp_local, slice_width)
    down_local = w_down.reshape(exp_local, slice_width, d_model)
    scaled = place * jnp.transpose(chosen, (1, 2, 0))[:, :, None, :]
    outgoing = jnp.einsum(
        "rjkt,td->rjkd", place, normed, preferred_element_type=jnp.float32
    ).astype(jnp.bfloat16)
    arrived = lax.all_to_all(outgoing, "row", split_axis=0, concat_axis=0, tiled=True)
    gate = jnp.einsum("qjkd,dje->qjke", arrived, gate_local, preferred_element_type=jnp.float32)
    upward = jnp.einsum("qjkd,dje->qjke", arrived, up_local, preferred_element_type=jnp.float32)
    act = (jax.nn.silu(gate) * upward).astype(jnp.bfloat16)
    returned = lax.all_to_all(
        jnp.einsum("qjke,jed->qjkd", act, down_local, preferred_element_type=jnp.float32).astype(
            jnp.bfloat16
        ),
        "row",
        split_axis=0,
        concat_axis=0,
        tiled=True,
    )
    mixture = lax.psum_scatter(
        jnp.einsum("rjkt,rjkd->td", scaled, returned, preferred_element_type=jnp.float32).astype(
            jnp.bfloat16
        ),
        "col",
        scatter_dimension=0,
        tiled=True,
    ).astype(jnp.float32)
    return (resid + mixture).astype(jnp.bfloat16)


def solution(mesh):
    return jax.shard_map(
        shards,
        mesh=mesh,
        in_specs=(
            P("row", None),
            P(("row", "col"), None, None),
            P(("row", "col"), None, None, None),
            P(("row", "col"), None, None, None),
            P("col", None),
            P(),
            P("row", None),
            P("row", None),
            P(None, ("row", "col")),
            P(None, ("row", "col")),
            P(("row", "col"), None),
        ),
        out_specs=P(("row", "col"), None),
        check_vma=False,
    )
```

```python
import functools
import math

import jax
import jax.numpy as jnp
from jax import lax
from jax.experimental import pallas as pl
from jax.experimental.pallas import tpu as pltpu
from jax.sharding import PartitionSpec as P

FF = 1024
CAP = 8
WIDTH = 512
SLOTS = 12


def fold(block):
    half = block.shape[1] // 2
    return jnp.concatenate([block[:, :half], block[:, half:]], axis=0).astype(jnp.bfloat16)


def unfold(block):
    block = block.astype(jnp.float32)
    half = block.shape[0] // 2
    return jnp.concatenate([block[:half], block[half:]], axis=1)


def layer(
    n_row, n_col, heads_ref, hidden_ref, gain_ref, chosen_ref, proj, w_gate, w_up, w_down, out_ref,
    ring, parts, blocks, picks, wide, normed, act, result, outbox, inbox, final, resid, load_sem,
    proj_sem, part_sem, block_sem, pick_sem, box_send, box_recv, final_sem,
):
    row, col = lax.axis_index("row"), lax.axis_index("col")
    rows = heads_ref.shape[0]
    depth = heads_ref.shape[1]
    model = hidden_ref.shape[1]
    count = act.shape[1] // WIDTH
    steps = model // WIDTH
    per_slot = ring.shape[1] // depth
    first = steps // per_slot

    def row_peer(off):
        return (lax.rem(row + off, n_row), col)

    def col_peer(off):
        return (row, lax.rem(col + off, n_col))

    def send(source, target, sems, off, peer):
        return pltpu.make_async_remote_copy(
            src_ref=source, dst_ref=target, send_sem=sems.at[0, off], recv_sem=sems.at[1, off],
            device_id=peer, device_id_type=pl.DeviceIdType.MESH,
        )

    def load_proj(j):
        slot, half = j // per_slot, j % per_slot
        return pltpu.make_async_copy(
            proj.at[:, pl.ds(j * WIDTH, WIDTH)],
            ring.at[slot, pl.ds(half * depth, depth)],
            proj_sem.at[j],
        )

    def load(weight, i, at):
        slot = lax.rem(at, SLOTS)
        start = pl.multiple_of(i * WIDTH, WIDTH)
        return pltpu.make_async_copy(
            weight.at[:, pl.ds(start, WIDTH)], ring.at[slot], load_sem.at[slot]
        )

    def load_gate(i):
        return load(w_gate, i, first + 2 * i)

    def load_up(i):
        return load(w_up, i, first + 2 * i + 1)

    def load_down(j):
        return load(w_down, j, first + 2 * count + j)

    for j in range(steps):
        load_proj(j).start()
    ready = (SLOTS - first) // 2
    for i in range(ready):
        load_gate(i).start()
        load_up(i).start()

    barrier = pltpu.get_barrier_semaphore()
    for off in range(1, n_row):
        pl.semaphore_signal(
            barrier, inc=1, device_id=row_peer(off), device_id_type=pl.DeviceIdType.MESH
        )
    for off in range(1, n_col):
        pl.semaphore_signal(
            barrier, inc=1, device_id=col_peer(off), device_id_type=pl.DeviceIdType.MESH
        )
    pl.semaphore_wait(barrier, n_row + n_col - 2)

    picks[0] = chosen_ref[...]
    sends = []
    for off in range(1, n_row):
        sends.append(send(picks.at[0], picks.at[off], pick_sem, off, row_peer(off)))
        sends[-1].start()

    for j in range(steps):
        load_proj(j).wait()
        slot, half = j // per_slot, j % per_slot
        resid[:, j * WIDTH : (j + 1) * WIDTH] = jnp.dot(
            heads_ref[...],
            ring[slot, half * depth : (half + 1) * depth],
            preferred_element_type=jnp.float32,
        )
    for i in range(ready, SLOTS // 2):
        load_gate(i).start()
        load_up(i).start()
    parts[0] = fold(resid[...])
    copies = []
    for off in range(1, n_col):
        copies.append(send(parts.at[0], parts.at[off], part_sem, off, col_peer(off)))
        copies[-1].start()
    sends += copies
    for copy in copies:
        copy.wait_recv()
    total = unfold(parts[0])
    for off in range(1, n_col):
        total = total + unfold(parts[off])
    total = total + hidden_ref[...].astype(jnp.float32)
    resid[...] = total
    scaled = total * lax.rsqrt(jnp.mean(total * total, axis=-1, keepdims=True) + 1e-06)
    blocks[0] = fold(scaled * gain_ref[...])
    copies = []
    for off in range(1, n_row):
        copies.append(send(blocks.at[0], blocks.at[off], block_sem, off, row_peer(off)))
        copies[-1].start()
    for copy in sends[: n_row - 1]:
        copy.wait_recv()
    sends += copies
    for off in range(n_row):
        if off:
            copies[off - 1].wait_recv()
        origin = lax.rem(row + n_row - off, n_row)
        wide[pl.ds(pl.multiple_of(origin * rows, rows), rows), :] = unfold(blocks[off])
    normed[...] = wide[...].astype(jnp.bfloat16)
    experts = picks.shape[2]
    weights = wide.at[:, pl.ds(0, experts)]
    for off in range(n_row):
        origin = lax.rem(row + n_row - off, n_row)
        weights[pl.ds(pl.multiple_of(origin * rows, rows), rows), :] = picks[off]

    def expert_step(i):
        load_gate(i).wait()
        gate = jnp.dot(
            normed[...], ring[lax.rem(first + 2 * i, SLOTS)], preferred_element_type=jnp.float32
        )
        load_up(i).wait()
        upward = jnp.dot(
            normed[...], ring[lax.rem(first + 2 * i + 1, SLOTS)], preferred_element_type=jnp.float32
        )
        expert = ((row * n_col + col) * act.shape[1] + i * WIDTH) // FF
        lane = lax.broadcasted_iota(jnp.int32, (wide.shape[0], experts), 1)
        scale = jnp.sum(
            jnp.where(lane == expert, wide[:, :experts], 0.0), axis=1, keepdims=True
        )
        value = gate / (1.0 + jnp.exp(-gate)) * upward * scale
        act[:, pl.ds(pl.multiple_of(i * WIDTH, WIDTH), WIDTH)] = value.astype(jnp.bfloat16)

    middle = count - SLOTS // 2
    last = (2 * count + steps - SLOTS) // 2

    @pl.loop(0, middle)
    def _(i):
        expert_step(i)
        load_gate(i + SLOTS // 2).start()
        load_up(i + SLOTS // 2).start()

    @pl.loop(middle, last)
    def _(i):
        expert_step(i)
        load_down(2 * (i - middle)).start()
        load_down(2 * (i - middle) + 1).start()

    @pl.loop(last, count)
    def _(i):
        expert_step(i)

    def box(off, j):
        return pltpu.make_async_remote_copy(
            src_ref=outbox.at[off, j], dst_ref=inbox.at[off, j],
            send_sem=box_send.at[off, j], recv_sem=box_recv.at[off, j],
            device_id=row_peer(off), device_id_type=pl.DeviceIdType.MESH,
        )

    @pl.loop(0, steps)
    def _(j):
        load_down(j).wait()
        result[...] = jnp.dot(
            act[...],
            ring[lax.rem(first + 2 * count + j, SLOTS)],
            preferred_element_type=jnp.float32,
        )
        for off in range(n_row):
            target = lax.rem(row + off, n_row)
            block = fold(result[pl.ds(pl.multiple_of(target * rows, rows), rows), :])
            if off:
                outbox[off, j] = block
                box(off, j).start()
            else:
                inbox[0, j] = block

    for j in range(steps):
        total = unfold(inbox[0, j])
        for off in range(1, n_row):
            box(off, j).wait_recv()
            total = total + unfold(inbox[off, j])
        wide[0:rows, j * WIDTH : (j + 1) * WIDTH] = total
    final[0] = fold(wide[0:rows, :])
    copies = []
    for off in range(1, n_col):
        copies.append(send(final.at[0], final.at[off], final_sem, off, col_peer(off)))
        copies[-1].start()
    sends += copies
    total = resid[...] + unfold(final[0])
    for off in range(1, n_col):
        copies[off - 1].wait_recv()
        total = total + unfold(final[off])
    out_ref[...] = total
    for copy in sends:
        copy.wait_send()
    for off in range(1, n_row):
        for j in range(steps):
            box(off, j).wait_send()


def fused(head_rows, hidden, norm_gain, chosen, proj, w_gate, w_up, w_down, n_row, n_col):
    rows, model = hidden.shape
    tokens = rows * n_row
    hid = w_gate.shape[1]
    steps = model // WIDTH
    experts = chosen.shape[1]
    vmem = pl.BlockSpec(memory_space=pltpu.VMEM)
    far = pl.BlockSpec(memory_space=pl.ANY)
    bf16, f32 = jnp.bfloat16, jnp.float32
    dma = pltpu.SemaphoreType.DMA
    flat = (2 * rows, model // 2)
    mini = (2 * rows, WIDTH // 2)
    weight_bytes = 2 * (proj.size + w_gate.size + w_up.size + w_down.size)
    return pl.pallas_call(
        functools.partial(layer, n_row, n_col),
        out_shape=jax.ShapeDtypeStruct((rows, model), f32),
        in_specs=[vmem] * 4 + [far] * 4,
        out_specs=vmem,
        scratch_shapes=[
            pltpu.VMEM((SLOTS, model, WIDTH), bf16),
            pltpu.VMEM((n_col,) + flat, bf16),
            pltpu.VMEM((n_row,) + flat, bf16),
            pltpu.VMEM((n_row, rows, experts), f32),
            pltpu.VMEM((tokens, model), f32),
            pltpu.VMEM((tokens, model), bf16),
            pltpu.VMEM((tokens, hid), bf16),
            pltpu.VMEM((tokens, WIDTH), f32),
            pltpu.VMEM((n_row, steps) + mini, bf16),
            pltpu.VMEM((n_row, steps) + mini, bf16),
            pltpu.VMEM((n_col,) + flat, bf16),
            pltpu.VMEM((rows, model), f32),
            dma((SLOTS,)),
            dma((steps,)),
            dma((2, n_col)),
            dma((2, n_row)),
            dma((2, n_row)),
            dma((n_row, steps)),
            dma((n_row, steps)),
            dma((2, n_col)),
        ],
        compiler_params=pltpu.CompilerParams(
            collective_id=0, has_side_effects=True, vmem_limit_bytes=60 * 2**20
        ),
        cost_estimate=pl.CostEstimate(
            flops=tokens * weight_bytes, bytes_accessed=weight_bytes, transcendentals=tokens * hid
        ),
    )(head_rows, hidden, norm_gain, chosen, proj, w_gate, w_up, w_down)


def normalize(resid, norm_gain):
    mean_square = jnp.mean(resid * resid, axis=-1, keepdims=True)
    return (resid * lax.rsqrt(mean_square + 1e-06) * norm_gain).astype(jnp.bfloat16)


def gather(block, axis, count):
    copies = jnp.broadcast_to(block[None], (count,) + block.shape)
    return lax.all_to_all(copies, axis, split_axis=0, concat_axis=0, tiled=True)


def shards(
    hidden, queries, keys, values, out_proj, norm_gain, routes, route_probs, w_gate, w_up, w_down
):
    row_count = lax.axis_size("row")
    col_count = lax.axis_size("col")
    col_id = lax.axis_index("col")
    tok_dev = queries.shape[0]
    heads = queries.shape[1]
    head_dim = queries.shape[2]
    kv_heads = keys.shape[1]
    group = heads // kv_heads
    d_model = w_gate.shape[0]
    hid_dev = w_gate.shape[1]
    grouped = queries.reshape(tok_dev, kv_heads, group, head_dim)
    scores = jnp.einsum(
        "tgqd,tgpd->tgqp", grouped, keys, preferred_element_type=jnp.float32
    ) / math.sqrt(head_dim)
    attn_weights = jax.nn.softmax(scores, axis=-1).astype(jnp.bfloat16)
    context = jnp.einsum(
        "tgqp,tgpd->tgqd", attn_weights, values, preferred_element_type=jnp.float32
    )
    context = context.astype(jnp.bfloat16).reshape(tok_dev, heads * head_dim)
    head_rows = lax.all_to_all(context, "col", split_axis=1, concat_axis=0, tiled=True)
    experts = hid_dev * row_count * col_count // FF
    slots_fit = d_model == hid_dev and d_model == 2 * head_rows.shape[1]
    if routes.shape[0] == CAP and slots_fit and experts % 128 == 0 and hid_dev == 8 * WIDTH:
        share = route_probs / jnp.sum(route_probs, axis=-1, keepdims=True)
        share = share.astype(jnp.bfloat16).astype(jnp.float32)
        chosen = jnp.sum(
            jnp.where(routes[:, :, None] == jnp.arange(experts), share[:, :, None], 0.0), axis=1
        )
        total = fused(
            head_rows, hidden, norm_gain[None], chosen, out_proj, w_gate, w_up, w_down,
            row_count, col_count,
        )
        return lax.dynamic_slice_in_dim(total, col_id * tok_dev, tok_dev, 0).astype(jnp.bfloat16)
    partial_sum = jnp.dot(head_rows, out_proj, preferred_element_type=jnp.float32)
    route_weight = (route_probs / jnp.sum(route_probs, axis=-1, keepdims=True)).astype(jnp.bfloat16)
    exp_local = max(1, hid_dev // FF)
    slice_width = hid_dev // exp_local
    dest_rows = jnp.arange(row_count, dtype=jnp.int32)
    experts_at = (dest_rows[:, None] * col_count + col_id) * hid_dev // FF
    experts_at = experts_at + jnp.arange(exp_local, dtype=jnp.int32)[None, :]
    match = routes[:, :, None, None] == experts_at[None, None, :, :]
    hits = jnp.any(match, axis=1).astype(jnp.int32)
    chosen = jnp.sum(
        jnp.where(match, route_weight[:, :, None, None], jnp.zeros((), jnp.bfloat16)), axis=1
    )
    if routes.shape[0] <= CAP:
        spread = lax.all_to_all(
            jnp.transpose(chosen, (1, 0, 2)).astype(jnp.float32),
            "row", split_axis=0, concat_axis=0, tiled=True,
        )
        spread = spread.reshape(row_count, col_count, tok_dev, exp_local)
        spread = jnp.transpose(spread, (1, 0, 2, 3)).reshape(-1, exp_local)
        parts = partial_sum.astype(jnp.bfloat16).reshape(col_count, tok_dev, d_model)
        parts = lax.all_to_all(parts, "col", split_axis=0, concat_axis=0, tiled=True)
        attn = jnp.sum(parts.astype(jnp.float32), axis=0)
        own = lax.dynamic_slice_in_dim(hidden, col_id * tok_dev, tok_dev, 0)
        resid = own.astype(jnp.float32) + attn
        normed = normalize(resid, norm_gain)
        normed = gather(gather(normed, "row", row_count).reshape(-1, d_model), "col", col_count)
        normed = normed.reshape(-1, d_model)
        gate = jnp.dot(normed, w_gate, preferred_element_type=jnp.float32)
        upward = jnp.dot(normed, w_up, preferred_element_type=jnp.float32)
        widen = jnp.arange(exp_local)[:, None] == jnp.arange(hid_dev)[None, :] // slice_width
        scale = jnp.dot(
            spread.astype(jnp.bfloat16),
            widen.astype(jnp.bfloat16),
            preferred_element_type=jnp.float32,
        )
        act = (jax.nn.silu(gate) * upward * scale).astype(jnp.bfloat16)
        down = jnp.dot(act, w_down, preferred_element_type=jnp.float32).astype(jnp.bfloat16)
        down = down.reshape(col_count, -1, d_model)
        down = lax.all_to_all(down, "col", split_axis=0, concat_axis=0, tiled=True)
        down = jnp.sum(down.astype(jnp.float32), axis=0).astype(jnp.bfloat16)
        down = down.reshape(row_count, tok_dev, d_model)
        down = lax.all_to_all(down, "row", split_axis=0, concat_axis=0, tiled=True)
        mixture = jnp.sum(down.astype(jnp.float32), axis=0)
        return (resid + mixture).astype(jnp.bfloat16)
    attn = lax.psum(partial_sum.astype(jnp.bfloat16), "col").astype(jnp.float32)
    row_resid = hidden.astype(jnp.float32) + attn
    normed = normalize(row_resid, norm_gain)
    resid = lax.dynamic_slice_in_dim(row_resid, col_id * tok_dev, tok_dev, 0)
    before = jnp.cumsum(hits, axis=0) - hits
    hits_t = jnp.transpose(hits, (1, 2, 0))
    before_t = jnp.transpose(before, (1, 2, 0))
    slot_ids = jnp.arange(CAP, dtype=jnp.int32)
    place = (hits_t[:, :, None, :] == 1) & (
        before_t[:, :, None, :] == slot_ids[None, None, :, None]
    )
    place = place.astype(jnp.bfloat16)
    gate_local = w_gate.reshape(d_model, exp_local, slice_width)
    up_local = w_up.reshape(d_model, exp_local, slice_width)
    down_local = w_down.reshape(exp_local, slice_width, d_model)
    scaled = place * jnp.transpose(chosen, (1, 2, 0))[:, :, None, :]
    outgoing = jnp.einsum(
        "rjkt,td->rjkd", place, normed, preferred_element_type=jnp.float32
    ).astype(jnp.bfloat16)
    arrived = lax.all_to_all(outgoing, "row", split_axis=0, concat_axis=0, tiled=True)
    gate = jnp.einsum("qjkd,dje->qjke", arrived, gate_local, preferred_element_type=jnp.float32)
    upward = jnp.einsum("qjkd,dje->qjke", arrived, up_local, preferred_element_type=jnp.float32)
    act = (jax.nn.silu(gate) * upward).astype(jnp.bfloat16)
    returned = lax.all_to_all(
        jnp.einsum("qjke,jed->qjkd", act, down_local, preferred_element_type=jnp.float32).astype(
            jnp.bfloat16
        ),
        "row",
        split_axis=0,
        concat_axis=0,
        tiled=True,
    )
    mixture = lax.psum_scatter(
        jnp.einsum("rjkt,rjkd->td", scaled, returned, preferred_element_type=jnp.float32).astype(
            jnp.bfloat16
        ),
        "col",
        scatter_dimension=0,
        tiled=True,
    ).astype(jnp.float32)
    return (resid + mixture).astype(jnp.bfloat16)


def solution(mesh):
    return jax.shard_map(
        shards,
        mesh=mesh,
        in_specs=(
            P("row", None),
            P(("row", "col"), None, None),
            P(("row", "col"), None, None, None),
            P(("row", "col"), None, None, None),
            P("col", None),
            P(),
            P("row", None),
            P("row", None),
            P(None, ("row", "col")),
            P(None, ("row", "col")),
            P(("row", "col"), None),
        ),
        out_specs=P(("row", "col"), None),
        check_vma=False,
    )
```

```python
import functools
import math

import jax
import jax.numpy as jnp
from jax import lax
from jax.experimental import pallas as pl
from jax.experimental.pallas import tpu as pltpu
from jax.sharding import PartitionSpec as P

FF = 1024
CAP = 8
WIDTH = 512
SLOTS = 12


def fold(block):
    half = block.shape[1] // 2
    return jnp.concatenate([block[:, :half], block[:, half:]], axis=0).astype(jnp.bfloat16)


def unfold(block):
    block = block.astype(jnp.float32)
    half = block.shape[0] // 2
    return jnp.concatenate([block[:half], block[half:]], axis=1)


def layer(
    n_row, n_col, experts, context_ref, hidden_ref, gain_ref, routes_ref, probs_ref, proj, w_gate, w_up, w_down, out_ref,
    ring, parts, blocks, picks, wide, normed, act, result, outbox, inbox, final, resid, load_sem,
    proj_sem, part_sem, block_sem, pick_sem, box_send, box_recv, final_sem, heads_in, heads, heads_sem,
):
    row, col = lax.axis_index("row"), lax.axis_index("col")
    rows, depth = heads.shape
    model = hidden_ref.shape[1]
    count = act.shape[1] // WIDTH
    steps = model // WIDTH
    per_slot = ring.shape[1] // depth
    first = steps // per_slot

    def row_peer(off):
        return (lax.rem(row + off, n_row), col)

    def col_peer(off):
        return (row, lax.rem(col + off, n_col))

    def send(source, target, sems, off, peer):
        return pltpu.make_async_remote_copy(
            src_ref=source, dst_ref=target, send_sem=sems.at[0, off], recv_sem=sems.at[1, off],
            device_id=peer, device_id_type=pl.DeviceIdType.MESH,
        )

    def load_proj(j):
        slot, half = j // per_slot, j % per_slot
        return pltpu.make_async_copy(
            proj.at[:, pl.ds(j * WIDTH, WIDTH)],
            ring.at[slot, pl.ds(half * depth, depth)],
            proj_sem.at[j],
        )

    def load(weight, i, at):
        slot = lax.rem(at, SLOTS)
        start = pl.multiple_of(i * WIDTH, WIDTH)
        return pltpu.make_async_copy(
            weight.at[:, pl.ds(start, WIDTH)], ring.at[slot], load_sem.at[slot]
        )

    def load_gate(i):
        return load(w_gate, i, first + 2 * i)

    def load_up(i):
        return load(w_up, i, first + 2 * i + 1)

    def load_down(j):
        return load(w_down, j, first + 2 * count + j)

    for j in range(steps):
        load_proj(j).start()
    ready = (SLOTS - first) // 2
    for i in range(ready):
        load_gate(i).start()
        load_up(i).start()

    barrier = pltpu.get_barrier_semaphore()
    for off in range(1, n_row):
        pl.semaphore_signal(
            barrier, inc=1, device_id=row_peer(off), device_id_type=pl.DeviceIdType.MESH
        )
    for off in range(1, n_col):
        pl.semaphore_signal(
            barrier, inc=1, device_id=col_peer(off), device_id_type=pl.DeviceIdType.MESH
        )
    pl.semaphore_wait(barrier, n_row + n_col - 2)

    heads_in[0] = context_ref[col]
    heads_copies = []
    for off in range(1, n_col):
        target = lax.rem(col + off, n_col)
        heads_copies.append(
            send(context_ref.at[target], heads_in.at[off], heads_sem, off, col_peer(off))
        )
        heads_copies[-1].start()
    share = probs_ref[...] / jnp.sum(probs_ref[...], axis=-1, keepdims=True)
    share = share.astype(jnp.bfloat16).astype(jnp.float32)
    lanes = lax.broadcasted_iota(jnp.int32, (rows, experts), 1)
    chosen = jnp.zeros((rows, experts), jnp.float32)
    for i in range(routes_ref.shape[1]):
        chosen = chosen + jnp.where(lanes == routes_ref[:, i : i + 1], share[:, i : i + 1], 0.0)
    picks[0] = chosen
    sends = []
    for off in range(1, n_row):
        sends.append(send(picks.at[0], picks.at[off], pick_sem, off, row_peer(off)))
        sends[-1].start()

    for copy in heads_copies:
        copy.wait_recv()
    own = rows // n_col
    piece = heads_in.shape[2]
    for origin in range(n_col):
        got = heads_in[lax.rem(col + n_col - origin, n_col)].astype(jnp.float32)
        for i in range(depth // piece):
            heads[origin * own : (origin + 1) * own, i * piece : (i + 1) * piece] = got[
                i * own : (i + 1) * own
            ]
    head_rows = heads[...].astype(jnp.bfloat16)
    for j in range(steps):
        load_proj(j).wait()
        slot, half = j // per_slot, j % per_slot
        resid[:, j * WIDTH : (j + 1) * WIDTH] = jnp.dot(
            head_rows,
            ring[slot, half * depth : (half + 1) * depth],
            preferred_element_type=jnp.float32,
        )
    for i in range(ready, SLOTS // 2):
        load_gate(i).start()
        load_up(i).start()
    parts[0] = fold(resid[...])
    copies = []
    for off in range(1, n_col):
        copies.append(send(parts.at[0], parts.at[off], part_sem, off, col_peer(off)))
        copies[-1].start()
    sends += copies
    for copy in copies:
        copy.wait_recv()
    total = unfold(parts[0])
    for off in range(1, n_col):
        total = total + unfold(parts[off])
    total = total + hidden_ref[...].astype(jnp.float32)
    resid[...] = total
    scaled = total * lax.rsqrt(jnp.mean(total * total, axis=-1, keepdims=True) + 1e-06)
    blocks[0] = fold(scaled * gain_ref[...])
    copies = []
    for off in range(1, n_row):
        copies.append(send(blocks.at[0], blocks.at[off], block_sem, off, row_peer(off)))
        copies[-1].start()
    for copy in sends[: n_row - 1]:
        copy.wait_recv()
    sends += copies
    for off in range(n_row):
        if off:
            copies[off - 1].wait_recv()
        origin = lax.rem(row + n_row - off, n_row)
        wide[pl.ds(pl.multiple_of(origin * rows, rows), rows), :] = unfold(blocks[off])
    normed[...] = wide[...].astype(jnp.bfloat16)
    weights = wide.at[:, pl.ds(0, experts)]
    for off in range(n_row):
        origin = lax.rem(row + n_row - off, n_row)
        weights[pl.ds(pl.multiple_of(origin * rows, rows), rows), :] = picks[off]

    def expert_step(i):
        load_gate(i).wait()
        gate = jnp.dot(
            normed[...], ring[lax.rem(first + 2 * i, SLOTS)], preferred_element_type=jnp.float32
        )
        load_up(i).wait()
        upward = jnp.dot(
            normed[...], ring[lax.rem(first + 2 * i + 1, SLOTS)], preferred_element_type=jnp.float32
        )
        expert = ((row * n_col + col) * act.shape[1] + i * WIDTH) // FF
        lane = lax.broadcasted_iota(jnp.int32, (wide.shape[0], experts), 1)
        scale = jnp.sum(
            jnp.where(lane == expert, wide[:, :experts], 0.0), axis=1, keepdims=True
        )
        value = gate / (1.0 + jnp.exp(-gate)) * upward * scale
        act[:, pl.ds(pl.multiple_of(i * WIDTH, WIDTH), WIDTH)] = value.astype(jnp.bfloat16)

    middle = count - SLOTS // 2
    last = (2 * count + steps - SLOTS) // 2

    @pl.loop(0, middle)
    def _(i):
        expert_step(i)
        load_gate(i + SLOTS // 2).start()
        load_up(i + SLOTS // 2).start()

    @pl.loop(middle, last)
    def _(i):
        expert_step(i)
        load_down(2 * (i - middle)).start()
        load_down(2 * (i - middle) + 1).start()

    @pl.loop(last, count)
    def _(i):
        expert_step(i)

    def box(off, j):
        return pltpu.make_async_remote_copy(
            src_ref=outbox.at[off, j], dst_ref=inbox.at[off, j],
            send_sem=box_send.at[off, j], recv_sem=box_recv.at[off, j],
            device_id=row_peer(off), device_id_type=pl.DeviceIdType.MESH,
        )

    @pl.loop(0, steps)
    def _(j):
        load_down(j).wait()
        result[...] = jnp.dot(
            act[...],
            ring[lax.rem(first + 2 * count + j, SLOTS)],
            preferred_element_type=jnp.float32,
        )
        for off in range(n_row):
            target = lax.rem(row + off, n_row)
            block = fold(result[pl.ds(pl.multiple_of(target * rows, rows), rows), :])
            if off:
                outbox[off, j] = block
                box(off, j).start()
            else:
                inbox[0, j] = block

    for j in range(steps):
        total = unfold(inbox[0, j])
        for off in range(1, n_row):
            box(off, j).wait_recv()
            total = total + unfold(inbox[off, j])
        wide[0:rows, j * WIDTH : (j + 1) * WIDTH] = total
    final[0] = fold(wide[0:rows, :])
    copies = []
    for off in range(1, n_col):
        copies.append(send(final.at[0], final.at[off], final_sem, off, col_peer(off)))
        copies[-1].start()
    sends += copies
    total = resid[...] + unfold(final[0])
    for off in range(1, n_col):
        copies[off - 1].wait_recv()
        total = total + unfold(final[off])
    out_ref[...] = total
    for copy in sends + heads_copies:
        copy.wait_send()
    for off in range(1, n_row):
        for j in range(steps):
            box(off, j).wait_send()


def fused(
    context, hidden, norm_gain, routes, probs, experts, proj, w_gate, w_up, w_down, n_row, n_col
):
    rows, model = hidden.shape
    tokens = rows * n_row
    hid = w_gate.shape[1]
    steps = model // WIDTH
    vmem = pl.BlockSpec(memory_space=pltpu.VMEM)
    far = pl.BlockSpec(memory_space=pl.ANY)
    bf16, f32 = jnp.bfloat16, jnp.float32
    dma = pltpu.SemaphoreType.DMA
    flat = (2 * rows, model // 2)
    mini = (2 * rows, WIDTH // 2)
    weight_bytes = 2 * (proj.size + w_gate.size + w_up.size + w_down.size)
    return pl.pallas_call(
        functools.partial(layer, n_row, n_col, experts),
        out_shape=jax.ShapeDtypeStruct((rows, model), f32),
        in_specs=[vmem] * 5 + [far] * 4,
        out_specs=vmem,
        scratch_shapes=[
            pltpu.VMEM((SLOTS, model, WIDTH), bf16),
            pltpu.VMEM((n_col,) + flat, bf16),
            pltpu.VMEM((n_row,) + flat, bf16),
            pltpu.VMEM((n_row, rows, experts), f32),
            pltpu.VMEM((tokens, model), f32),
            pltpu.VMEM((tokens, model), bf16),
            pltpu.VMEM((tokens, hid), bf16),
            pltpu.VMEM((tokens, WIDTH), f32),
            pltpu.VMEM((n_row, steps) + mini, bf16),
            pltpu.VMEM((n_row, steps) + mini, bf16),
            pltpu.VMEM((n_col,) + flat, bf16),
            pltpu.VMEM((rows, model), f32),
            dma((SLOTS,)),
            dma((steps,)),
            dma((2, n_col)),
            dma((2, n_row)),
            dma((2, n_row)),
            dma((n_row, steps)),
            dma((n_row, steps)),
            dma((2, n_col)),
            pltpu.VMEM(context.shape, bf16),
            pltpu.VMEM((rows, proj.shape[0]), f32),
            dma((2, n_col)),
        ],
        compiler_params=pltpu.CompilerParams(
            collective_id=0, has_side_effects=True, vmem_limit_bytes=60 * 2**20
        ),
        cost_estimate=pl.CostEstimate(
            flops=tokens * weight_bytes, bytes_accessed=weight_bytes, transcendentals=tokens * hid
        ),
    )(context, hidden, norm_gain, routes, probs, proj, w_gate, w_up, w_down)


def normalize(resid, norm_gain):
    mean_square = jnp.mean(resid * resid, axis=-1, keepdims=True)
    return (resid * lax.rsqrt(mean_square + 1e-06) * norm_gain).astype(jnp.bfloat16)


def gather(block, axis, count):
    copies = jnp.broadcast_to(block[None], (count,) + block.shape)
    return lax.all_to_all(copies, axis, split_axis=0, concat_axis=0, tiled=True)


def shards(
    hidden, queries, keys, values, out_proj, norm_gain, routes, route_probs, w_gate, w_up, w_down
):
    row_count = lax.axis_size("row")
    col_count = lax.axis_size("col")
    col_id = lax.axis_index("col")
    tok_dev = queries.shape[0]
    heads = queries.shape[1]
    head_dim = queries.shape[2]
    kv_heads = keys.shape[1]
    group = heads // kv_heads
    d_model = w_gate.shape[0]
    hid_dev = w_gate.shape[1]
    grouped = queries.reshape(tok_dev, kv_heads, group, head_dim)
    scores = jnp.einsum(
        "tgqd,tgpd->tgqp", grouped, keys, preferred_element_type=jnp.float32
    ) / math.sqrt(head_dim)
    attn_weights = jax.nn.softmax(scores, axis=-1).astype(jnp.bfloat16)
    context = jnp.einsum(
        "tgqp,tgpd->tgqd", attn_weights, values, preferred_element_type=jnp.float32
    )
    context = context.astype(jnp.bfloat16).reshape(tok_dev, heads * head_dim)
    experts = hid_dev * row_count * col_count // FF
    slots_fit = d_model == hid_dev and d_model == 2 * out_proj.shape[0]
    if routes.shape[0] == CAP and slots_fit and experts % 128 == 0 and hid_dev == 8 * WIDTH:
        own = routes.shape[0] // col_count
        cut = context.reshape(own, col_count, 16 // own, -1)
        cut = jnp.transpose(cut, (1, 2, 0, 3)).reshape(col_count, 16, -1)
        total = fused(
            cut, hidden, norm_gain[None], routes, route_probs, experts, out_proj, w_gate, w_up, w_down,
            row_count, col_count,
        )
        return lax.dynamic_slice_in_dim(total, col_id * tok_dev, tok_dev, 0).astype(jnp.bfloat16)
    head_rows = lax.all_to_all(context, "col", split_axis=1, concat_axis=0, tiled=True)
    partial_sum = jnp.dot(head_rows, out_proj, preferred_element_type=jnp.float32)
    route_weight = (route_probs / jnp.sum(route_probs, axis=-1, keepdims=True)).astype(jnp.bfloat16)
    exp_local = max(1, hid_dev // FF)
    slice_width = hid_dev // exp_local
    dest_rows = jnp.arange(row_count, dtype=jnp.int32)
    experts_at = (dest_rows[:, None] * col_count + col_id) * hid_dev // FF
    experts_at = experts_at + jnp.arange(exp_local, dtype=jnp.int32)[None, :]
    match = routes[:, :, None, None] == experts_at[None, None, :, :]
    hits = jnp.any(match, axis=1).astype(jnp.int32)
    chosen = jnp.sum(
        jnp.where(match, route_weight[:, :, None, None], jnp.zeros((), jnp.bfloat16)), axis=1
    )
    if routes.shape[0] <= CAP:
        spread = lax.all_to_all(
            jnp.transpose(chosen, (1, 0, 2)).astype(jnp.float32),
            "row", split_axis=0, concat_axis=0, tiled=True,
        )
        spread = spread.reshape(row_count, col_count, tok_dev, exp_local)
        spread = jnp.transpose(spread, (1, 0, 2, 3)).reshape(-1, exp_local)
        parts = partial_sum.astype(jnp.bfloat16).reshape(col_count, tok_dev, d_model)
        parts = lax.all_to_all(parts, "col", split_axis=0, concat_axis=0, tiled=True)
        attn = jnp.sum(parts.astype(jnp.float32), axis=0)
        own = lax.dynamic_slice_in_dim(hidden, col_id * tok_dev, tok_dev, 0)
        resid = own.astype(jnp.float32) + attn
        normed = normalize(resid, norm_gain)
        normed = gather(gather(normed, "row", row_count).reshape(-1, d_model), "col", col_count)
        normed = normed.reshape(-1, d_model)
        gate = jnp.dot(normed, w_gate, preferred_element_type=jnp.float32)
        upward = jnp.dot(normed, w_up, preferred_element_type=jnp.float32)
        widen = jnp.arange(exp_local)[:, None] == jnp.arange(hid_dev)[None, :] // slice_width
        scale = jnp.dot(
            spread.astype(jnp.bfloat16),
            widen.astype(jnp.bfloat16),
            preferred_element_type=jnp.float32,
        )
        act = (jax.nn.silu(gate) * upward * scale).astype(jnp.bfloat16)
        down = jnp.dot(act, w_down, preferred_element_type=jnp.float32).astype(jnp.bfloat16)
        down = down.reshape(col_count, -1, d_model)
        down = lax.all_to_all(down, "col", split_axis=0, concat_axis=0, tiled=True)
        down = jnp.sum(down.astype(jnp.float32), axis=0).astype(jnp.bfloat16)
        down = down.reshape(row_count, tok_dev, d_model)
        down = lax.all_to_all(down, "row", split_axis=0, concat_axis=0, tiled=True)
        mixture = jnp.sum(down.astype(jnp.float32), axis=0)
        return (resid + mixture).astype(jnp.bfloat16)
    attn = lax.psum(partial_sum.astype(jnp.bfloat16), "col").astype(jnp.float32)
    row_resid = hidden.astype(jnp.float32) + attn
    normed = normalize(row_resid, norm_gain)
    resid = lax.dynamic_slice_in_dim(row_resid, col_id * tok_dev, tok_dev, 0)
    before = jnp.cumsum(hits, axis=0) - hits
    hits_t = jnp.transpose(hits, (1, 2, 0))
    before_t = jnp.transpose(before, (1, 2, 0))
    slot_ids = jnp.arange(CAP, dtype=jnp.int32)
    place = (hits_t[:, :, None, :] == 1) & (
        before_t[:, :, None, :] == slot_ids[None, None, :, None]
    )
    place = place.astype(jnp.bfloat16)
    gate_local = w_gate.reshape(d_model, exp_local, slice_width)
    up_local = w_up.reshape(d_model, exp_local, slice_width)
    down_local = w_down.reshape(exp_local, slice_width, d_model)
    scaled = place * jnp.transpose(chosen, (1, 2, 0))[:, :, None, :]
    outgoing = jnp.einsum(
        "rjkt,td->rjkd", place, normed, preferred_element_type=jnp.float32
    ).astype(jnp.bfloat16)
    arrived = lax.all_to_all(outgoing, "row", split_axis=0, concat_axis=0, tiled=True)
    gate = jnp.einsum("qjkd,dje->qjke", arrived, gate_local, preferred_element_type=jnp.float32)
    upward = jnp.einsum("qjkd,dje->qjke", arrived, up_local, preferred_element_type=jnp.float32)
    act = (jax.nn.silu(gate) * upward).astype(jnp.bfloat16)
    returned = lax.all_to_all(
        jnp.einsum("qjke,jed->qjkd", act, down_local, preferred_element_type=jnp.float32).astype(
            jnp.bfloat16
        ),
        "row",
        split_axis=0,
        concat_axis=0,
        tiled=True,
    )
    mixture = lax.psum_scatter(
        jnp.einsum("rjkt,rjkd->td", scaled, returned, preferred_element_type=jnp.float32).astype(
            jnp.bfloat16
        ),
        "col",
        scatter_dimension=0,
        tiled=True,
    ).astype(jnp.float32)
    return (resid + mixture).astype(jnp.bfloat16)


def solution(mesh):
    return jax.shard_map(
        shards,
        mesh=mesh,
        in_specs=(
            P("row", None),
            P(("row", "col"), None, None),
            P(("row", "col"), None, None, None),
            P(("row", "col"), None, None, None),
            P("col", None),
            P(),
            P("row", None),
            P("row", None),
            P(None, ("row", "col")),
            P(None, ("row", "col")),
            P(("row", "col"), None),
        ),
        out_specs=P(("row", "col"), None),
        check_vma=False,
    )
```
